128 devices in a mesh: ctx: 16 (over z_lo, x, core), tp: 8 (over z_hi, y).
Axes of the slice: x: 4, y: 4, z: 4 (z_hi: 2, z_lo: 2; z = z_hi * 2 + z_lo), core: 2. Of those that a mesh axis runs over, the one named last changes fastest.
Arguments:
- query_proj: float32 [6144, 8192], P('ctx', 'tp'), may hold values from -6 to 6
- key_proj: float32 [6144, 8192], P('ctx', 'tp'), may hold values from -6 to 6
- value_proj: float32 [6144, 8192], P('ctx', 'tp'), may hold values from -6 to 6
- short_taps: float32 [3, 3, 8192], P(None, None, 'tp'), may hold values from -4 to 4
- pole_rates: float32 [16, 8192], P(None, 'tp'), may hold values from 1.6276042e-06 to 0.05
- residues: float32 [16, 8192], P(None, 'tp'), may hold values from -0.06 to 0.06
- skip_gain: float32 [8192], P('tp'), may hold values from -3 to 3
- out_weight: bfloat16 [8192, 8192], P('tp', 'ctx'), may hold values from -0.09375 to 0.09375
Outputs:
- block_out: float32 [6144, 8192], P('ctx', 'tp')
The draws below stay inside these ranges and needn't reach their ends.
All inputs are finite; a program needn't handle non-finite values.
Results may differ from the reference program's by a relative error of at most 0.0029.
Values may be sent and summed in bfloat16 or wider, within the bound.
No kernel may reach another device: no remote copies, remote signals or barrier semaphores. Data moves between devices by JAX's collectives and lax.ppermute only.
A program may use at most 128 MiB of HBM per device.

```python
import math
import jax
import jax.numpy as jnp
import numpy as np
from jax import lax

D = 8192
MODES = 16
SHORT = 3
TOKENS = 6144


def raised(values, rng, source, target, parts, factor):
    def block_of(axis_at):
        return (jnp.arange(values.shape[axis_at]) // (values.shape[axis_at] // parts)).reshape((-1,) + (1,) * (values.ndim - 1 - axis_at))

    first = jax.random.permutation(rng, parts)[block_of(target)]
    other_side = (block_of(target) + parts // 2) % parts
    return jnp.where((block_of(source) == first) | (block_of(source) == other_side), factor * values, values)


def block_levels(key, extent, cuts, least, high):
    level, own = 1.0, jax.random.fold_in(key, 6)
    for axis_at, shards_of in cuts:
        draws = jnp.exp(jax.random.uniform(jax.random.fold_in(own, axis_at), (shards_of,), jnp.float32, least / len(cuts), high / len(cuts)))
        level = level * jnp.repeat(draws, extent[axis_at] // shards_of).reshape([-1 if axis == axis_at else 1 for axis in range(len(extent))])
    return level


def bell_draw(key, dims, scale, limit, cuts=(), kind=jnp.bfloat16):
    drawn = jax.random.normal(key, dims, jnp.float32) * scale
    if len(cuts) > 0:
        drawn = block_levels(key, dims, cuts, -0.22, 0.18) * drawn
    return jnp.clip(drawn, min=-limit, max=limit).astype(kind)


def heavy_noise(own_key, shape, width, bound, pieces, heavy, kind=jnp.bfloat16):
    entries = width * jax.random.normal(own_key, shape, jnp.float32)
    if pieces:
        entries = entries * block_levels(own_key, shape, pieces, -0.22, 0.18)
    return jnp.clip(raised(entries, jax.random.fold_in(own_key, 3), *heavy), -bound, bound).astype(kind)


def setup_inputs(seed: int = 0) -> dict:
    keys = jax.random.split(jax.random.key(seed), 9)
    return {
        "query_proj": bell_draw(keys[0], (TOKENS, D), 1.0, 6.0, ((0, 16), (1, 8)), jnp.float32),
        "key_proj": bell_draw(keys[1], (TOKENS, D), 1.0, 6.0, ((0, 16), (1, 8)), jnp.float32),
        "value_proj": bell_draw(keys[2], (TOKENS, D), 1.0, 6.0, ((0, 16), (1, 8)), jnp.float32),
        "short_taps": bell_draw(keys[3], (3, SHORT, D), 0.6, 4.0, ((2, 8),), jnp.float32),
        "pole_rates": jnp.clip(jnp.exp(math.log(0.05) - 10.332669 * jax.random.uniform(keys[4], (MODES, D), jnp.float32) ** block_levels(keys[4], (MODES, D), ((1, 8),), -0.2, 0.2)), 1.6276042060781037e-06, 0.05),
        "residues": bell_draw(keys[5], (MODES, D), 0.01, 0.06, ((1, 8),), jnp.float32),
        "skip_gain": bell_draw(keys[6], (D,), 0.5, 3.0, ((0, 8),), jnp.float32),
        "out_weight": heavy_noise(keys[7], (D, D), D ** -0.5, 0.09375, ((0, 8), (1, 16)), (0, 1, 16, 2.0)),
    }


HI = lax.Precision.HIGHEST


def short_filter(signal, tap_set):
    padded = jnp.pad(signal, ((2, 0), (0, 0)))
    return tap_set[0] * signal + tap_set[1] * padded[1:-1] + tap_set[2] * padded[:-2]


def modal_blocks(forcing, decays, residues, modal_state):
    block_len = 32
    steps_at = jnp.arange(block_len, dtype=jnp.float32)
    powers = jnp.exp(-decays[None] * steps_at[:, None, None])
    lead_powers = powers * jnp.exp(-decays)[None]
    behind = powers[::-1]
    kernel = jnp.einsum("tmc,mc->tc", powers, residues, precision=HI)
    offset_grid = np.arange(block_len)[:, None] - np.arange(block_len)[None, :]
    toeplitz = jnp.where((offset_grid >= 0)[:, :, None], kernel[np.clip(offset_grid, 0, None)], 0.0)
    weighted = lead_powers * residues[None]
    block_decay = jnp.exp(-decays * block_len)
    blocks = forcing.reshape(-1, block_len, forcing.shape[1])

    def advance(carried, block):
        produced = jnp.einsum("tsc,sc->tc", toeplitz, block, precision=HI)
        produced = produced + jnp.einsum("tmc,mc->tc", weighted, carried, precision=HI)
        carried = block_decay * carried + jnp.einsum("tmc,tc->mc", behind, block, precision=HI)
        return carried, produced

    last_state, outputs = lax.scan(advance, modal_state, blocks)
    return last_state, outputs.reshape(forcing.shape)


def reference(query_proj, key_proj, value_proj, short_taps, pole_rates, residues, skip_gain, out_weight):
    query_feat = short_filter(query_proj, short_taps[0])
    key_feat = short_filter(key_proj, short_taps[1])
    value_feat = short_filter(value_proj, short_taps[2])
    gated_input = key_feat * value_feat
    start_state = jnp.zeros(pole_rates.shape, jnp.float32)
    last_state, convolved = modal_blocks(gated_input, pole_rates, residues, start_state)
    convolved = convolved + skip_gain[None] * gated_input
    hidden = (query_feat * convolved).astype(jnp.bfloat16)
    return jnp.dot(hidden, out_weight, preferred_element_type=jnp.float32)
```

```python
import functools
import itertools

import jax
import jax.numpy as jnp
from jax import lax
from jax.experimental import pallas as pl
from jax.experimental.pallas import tpu as pltpu
from jax.sharding import Mesh, PartitionSpec as P

AXES = ("zl", "x", "core", "zh", "y")
SIZES = {"zl": 2, "x": 4, "core": 2, "zh": 2, "y": 4}
CTX = ("zl", "x", "core")
TP = ("zh", "y")
SEGS = 8
LANES = 128


def coords(axes):
    for values in itertools.product(*[range(SIZES[a]) for a in axes]):
        yield dict(zip(axes, values))


def place(axes, at):
    index = 0
    for a in axes:
        index = index * SIZES[a] + at[a]
    return index


def permute(value, axes, move):
    pairs = [(place(axes, at), place(axes, move(at))) for at in coords(axes)]
    return lax.ppermute(value, axes, pairs)


def moved(value, axis, by):
    return permute(value, (axis,), lambda at: {axis: (at[axis] + by) % SIZES[axis]})


def onward(value, axis):
    axes = tuple(a for a in AXES if a in (axis, "core"))

    def move(at):
        step = 1 if at["core"] == 0 else -1
        return {**at, axis: (at[axis] + step) % SIZES[axis]}

    return permute(value, axes, move)


def turned(value):
    def move(at):
        return {
            "zl": at["zh"],
            "x": (2 * at["x"] - at["y"]) % 4,
            "core": at["core"],
            "zh": at["zl"],
            "y": at["x"],
        }

    return permute(value, AXES, move)


def later(value, by):
    size = 16
    return lax.ppermute(value, CTX, [(i, i + by) for i in range(size - by)])


def rows_of(ref, j, seg_len):
    return ref[pl.ds(j, SEGS, stride=seg_len), :]


def local_kernel(seg_len, modes, q_ref, k_ref, v_ref, halo_ref, taps_ref, rates_ref, res_ref, skip_ref, y_ref, qf_ref, total_ref, carry_ref):
    wide = (SEGS, LANES)
    sub = lax.broadcasted_iota(jnp.int32, wide, 0)
    rates = rates_ref[...]
    pole = jnp.exp(-rates)

    def spread(row):
        return jnp.broadcast_to(row, wide)

    taps = [[spread(taps_ref[3 * a + b : 3 * a + b + 1, :]) for b in range(3)] for a in range(3)]
    skip = spread(skip_ref[...])
    poles = [spread(pole[m : m + 1, :]) for m in range(modes)]
    gains = [spread(res_ref[m : m + 1, :]) for m in range(modes)]

    def before(ref, back, halo_row):
        rolled = pltpu.roll(rows_of(ref, seg_len - back, seg_len), 1, 0)
        return jnp.where(sub == 0, spread(halo_ref[halo_row : halo_row + 1, :]), rolled)

    refs = (q_ref, k_ref, v_ref)
    past = tuple((before(ref, 1, 2 * a + 1), before(ref, 2, 2 * a)) for a, ref in enumerate(refs))

    def step(j, carried):
        past, states = carried
        feats, new_past = [], []
        for a, ref in enumerate(refs):
            now = rows_of(ref, j, seg_len)
            one, two = past[a]
            feats.append(taps[a][0] * now + taps[a][1] * one + taps[a][2] * two)
            new_past.append((now, one))
        gated = feats[1] * feats[2]
        parts = [skip * gated, None, None, None]
        new_states = []
        for m in range(modes):
            state = poles[m] * states[m] + gated
            new_states.append(state)
            term = gains[m] * state
            parts[m % 4] = term if parts[m % 4] is None else parts[m % 4] + term
        y_ref[j] = (parts[0] + parts[1]) + (parts[2] + parts[3])
        qf_ref[j] = feats[0]
        return tuple(new_past), tuple(new_states)

    zeros = tuple(jnp.zeros(wide, jnp.float32) for _ in range(modes))
    _, ends = lax.fori_loop(0, seg_len, step, (past, zeros), unroll=4)

    seg = jnp.exp(-float(seg_len) * rates)
    for m in range(modes):
        power = spread(seg[m : m + 1, :])
        run = ends[m]
        for by in (1, 2, 4):
            run = run + jnp.where(sub >= by, power * pltpu.roll(run, by, 0), 0.0)
            power = power * power
        total_ref[m : m + 1, :] = run[SEGS - 1 : SEGS, :]
        carry_ref[m] = jnp.where(sub >= 1, pltpu.roll(run, 1, 0), 0.0)


def finish_kernel(seg_len, modes, y_ref, qf_ref, carry_ref, entering_ref, rates_ref, res_ref, hidden_ref, rows_ref):
    wide = (SEGS, LANES)
    sub = lax.broadcasted_iota(jnp.int32, wide, 0).astype(jnp.float32)
    rates = rates_ref[...]
    pole = jnp.exp(-rates)
    poles, starts = [], []
    for m in range(modes):
        rate = jnp.broadcast_to(rates[m : m + 1, :], wide)
        come = jnp.exp(-float(seg_len) * sub * rate) * jnp.broadcast_to(entering_ref[m : m + 1, :], wide)
        poles.append(jnp.broadcast_to(pole[m : m + 1, :], wide))
        starts.append(jnp.broadcast_to(res_ref[m : m + 1, :], wide) * (carry_ref[m] + come))

    def step(j, states):
        parts = [y_ref[j], None, None, None]
        new_states = []
        for m in range(modes):
            state = poles[m] * states[m]
            new_states.append(state)
            parts[m % 4] = state if parts[m % 4] is None else parts[m % 4] + state
        rows_ref[pl.ds(j, SEGS, stride=seg_len), :] = qf_ref[j] * ((parts[0] + parts[1]) + (parts[2] + parts[3]))
        return tuple(new_states)

    lax.fori_loop(0, seg_len, step, tuple(starts), unroll=4)
    hidden_ref[...] = rows_ref[...].astype(jnp.bfloat16)


def local_part(q, k, v, halo, taps, rates, res, skip):
    rows, channels = q.shape
    modes = rates.shape[0]
    seg_len = rows // SEGS
    tall = pl.BlockSpec((rows, LANES), lambda c: (0, c))

    def short(n):
        return pl.BlockSpec((n, LANES), lambda c: (0, c))

    cube = pl.BlockSpec((seg_len, SEGS, LANES), lambda c: (0, 0, c))
    mode_cube = pl.BlockSpec((modes, SEGS, LANES), lambda c: (0, 0, c))
    f32 = jnp.float32
    return pl.pallas_call(
        functools.partial(local_kernel, seg_len, modes),
        grid=(channels // LANES,),
        in_specs=[tall, tall, tall, short(6), short(9), short(modes), short(modes), short(1)],
        out_specs=[cube, cube, short(modes), mode_cube],
        out_shape=[
            jax.ShapeDtypeStruct((seg_len, SEGS, channels), f32),
            jax.ShapeDtypeStruct((seg_len, SEGS, channels), f32),
            jax.ShapeDtypeStruct((modes, channels), f32),
            jax.ShapeDtypeStruct((modes, SEGS, channels), f32),
        ],
        compiler_params=pltpu.CompilerParams(vmem_limit_bytes=24 * 2**20),
        cost_estimate=pl.CostEstimate(flops=40_000_000, bytes_accessed=9_000_000, transcendentals=0),
        name="local_part",
    )(q, k, v, halo, taps, rates, res, skip)


def finish_part(y, qf, carry, entering, rates, res):
    seg_len, _, channels = y.shape
    modes = rates.shape[0]
    rows = seg_len * SEGS

    def short(n):
        return pl.BlockSpec((n, LANES), lambda c: (0, c))

    cube = pl.BlockSpec((seg_len, SEGS, LANES), lambda c: (0, 0, c))
    mode_cube = pl.BlockSpec((modes, SEGS, LANES), lambda c: (0, 0, c))
    return pl.pallas_call(
        functools.partial(finish_kernel, seg_len, modes),
        grid=(channels // LANES,),
        in_specs=[cube, cube, mode_cube, short(modes), short(modes), short(modes)],
        out_specs=pl.BlockSpec((rows, LANES), lambda c: (0, c)),
        out_shape=jax.ShapeDtypeStruct((rows, channels), jnp.bfloat16),
        scratch_shapes=[pltpu.VMEM((rows, LANES), jnp.float32)],
        compiler_params=pltpu.CompilerParams(vmem_limit_bytes=24 * 2**20),
        cost_estimate=pl.CostEstimate(flops=15_000_000, bytes_accessed=4_000_000, transcendentals=0),
        name="finish_part",
    )(y, qf, carry, entering, rates, res)


def pick(first, second):
    return jnp.where(lax.axis_index("core") == 0, first, second)


def spread_over(own, ring, pair):
    got = {(0, 0): own}
    got[0, -1] = moved(own, ring, 1)
    got[0, 1] = moved(own, ring, -1)
    got[1, 0] = moved(own, pair, 1)
    got[0, 2] = onward(pick(got[0, -1], got[0, 1]), ring)
    got[1, -1] = moved(got[1, 0], ring, 1)
    got[1, 1] = moved(got[1, 0], ring, -1)
    got[1, 2] = onward(pick(got[1, -1], got[1, 1]), ring)
    return got


def on_device(q, k, v, short_taps, rates, res, skip, weight):
    channels = rates.shape[1]
    halo = later(jnp.concatenate([q[-2:], k[-2:], v[-2:]], axis=0), 1)
    block = turned(weight)
    y, qf, total, carry = local_part(
        q, k, v, halo, short_taps.reshape(9, channels), rates, res, skip.reshape(1, channels)
    )
    rows = q.shape[0]

    def device_decay(times):
        return jnp.exp(-rates * float(rows * times))

    near = later(total, 1) + device_decay(1) * later(total, 2) + device_decay(2) * later(total, 3)
    window = total + device_decay(1) * near
    entering = (
        near
        + device_decay(3) * later(window, 4)
        + device_decay(7) * later(window, 8)
        + device_decay(11) * later(window, 12)
    )
    hidden = finish_part(y, qf, carry, entering, rates, res)

    weights = spread_over(block, "x", "zl")
    hiddens = spread_over(hidden, "y", "zh")

    slots = [(a, b) for a in (0, 1) for b in (0, 1, 2, -1)]
    held = jnp.stack([hiddens[s] for s in slots])
    flip = (lax.axis_index("zh") + lax.axis_index("zl")) % 2
    turn = lax.axis_index("y") - lax.axis_index("x")
    own = jnp.zeros((rows, weight.shape[1]), jnp.float32)
    other = jnp.zeros((rows, weight.shape[1]), jnp.float32)
    for a, b in slots:
        swapped = moved(weights[a, b], "core", 1)
        slot = ((a + flip) % 2) * 4 + (turn - b) % 4
        term = lax.dynamic_index_in_dim(held, slot, 0, keepdims=False)
        own = own + jnp.dot(term, weights[a, b], preferred_element_type=jnp.float32)
        other = other + jnp.dot(term, swapped, preferred_element_type=jnp.float32)
    first = lax.axis_index("core") == 0
    return jnp.concatenate([jnp.where(first, own, other), jnp.where(first, other, own)], axis=1)


def solution(mesh):
    fine = Mesh(mesh.devices.reshape(tuple(SIZES[a] for a in AXES)), AXES)
    in_specs = (
        P(CTX, TP),
        P(CTX, TP),
        P(CTX, TP),
        P(None, None, TP),
        P(None, TP),
        P(None, TP),
        P(TP),
        P(TP, CTX),
    )
    return jax.shard_map(on_device, mesh=fine, in_specs=in_specs, out_specs=P(CTX, TP), check_vma=False)
```

```python
import functools
import itertools

import jax
import jax.numpy as jnp
from jax import lax
from jax.experimental import pallas as pl
from jax.experimental.pallas import tpu as pltpu
from jax.sharding import Mesh, PartitionSpec as P

AXES = ("zl", "x", "core", "zh", "y")
SIZES = {"zl": 2, "x": 4, "core": 2, "zh": 2, "y": 4}
CTX = ("zl", "x", "core")
TP = ("zh", "y")
SEGS = 8
LANES = 128


def coords(axes):
    for values in itertools.product(*[range(SIZES[a]) for a in axes]):
        yield dict(zip(axes, values))


def place(axes, at):
    index = 0
    for a in axes:
        index = index * SIZES[a] + at[a]
    return index


def permute(value, axes, move):
    pairs = [(place(axes, at), place(axes, move(at))) for at in coords(axes)]
    return lax.ppermute(value, axes, pairs)


def moved(value, axis, by):
    return permute(value, (axis,), lambda at: {axis: (at[axis] + by) % SIZES[axis]})


def onward(value, axis):
    axes = tuple(a for a in AXES if a in (axis, "core"))

    def move(at):
        step = 1 if at["core"] == 0 else -1
        return {**at, axis: (at[axis] + step) % SIZES[axis]}

    return permute(value, axes, move)


def turned(value):
    def move(at):
        return {
            "zl": at["zh"],
            "x": (2 * at["x"] - at["y"]) % 4,
            "core": at["core"],
            "zh": at["zl"],
            "y": at["x"],
        }

    return permute(value, AXES, move)


def tie(*values):
    return lax.optimization_barrier(values)


def rows_of(ref, j, seg_len):
    return ref[pl.ds(j, SEGS, stride=seg_len), :]


def local_kernel(seg_len, modes, q_ref, k_ref, v_ref, halo_ref, taps_ref, rates_ref, res_ref, skip_ref, y_ref, qf_ref, total_ref, carry_ref):
    wide = (SEGS, LANES)
    sub = lax.broadcasted_iota(jnp.int32, wide, 0)
    rates = rates_ref[...]
    pole = jnp.exp(-rates)

    def spread(row):
        return jnp.broadcast_to(row, wide)

    taps = [[spread(taps_ref[a, b : b + 1, :]) for b in range(3)] for a in range(3)]
    skip = spread(skip_ref[...])
    poles = [spread(pole[m : m + 1, :]) for m in range(modes)]
    gains = [spread(res_ref[m : m + 1, :]) for m in range(modes)]

    def before(ref, back, halo_row):
        rolled = pltpu.roll(rows_of(ref, seg_len - back, seg_len), 1, 0)
        return jnp.where(sub == 0, spread(halo_ref[halo_row : halo_row + 1, :]), rolled)

    refs = (q_ref, k_ref, v_ref)
    past = tuple((before(ref, 1, 8 * a + 7), before(ref, 2, 8 * a + 6)) for a, ref in enumerate(refs))

    def step(j, carried):
        past, states = carried
        feats, new_past = [], []
        for a, ref in enumerate(refs):
            now = rows_of(ref, j, seg_len)
            one, two = past[a]
            feats.append(taps[a][0] * now + taps[a][1] * one + taps[a][2] * two)
            new_past.append((now, one))
        gated = feats[1] * feats[2]
        parts = [skip * gated, None, None, None]
        new_states = []
        for m in range(modes):
            state = poles[m] * states[m] + gated
            new_states.append(state)
            term = gains[m] * state
            parts[m % 4] = term if parts[m % 4] is None else parts[m % 4] + term
        y_ref[j] = (parts[0] + parts[1]) + (parts[2] + parts[3])
        qf_ref[j] = feats[0]
        return tuple(new_past), tuple(new_states)

    zeros = tuple(jnp.zeros(wide, jnp.float32) for _ in range(modes))
    _, ends = lax.fori_loop(0, seg_len, step, (past, zeros), unroll=4)

    seg = jnp.exp(-float(seg_len) * rates)
    for m in range(modes):
        power = spread(seg[m : m + 1, :])
        run = ends[m]
        for by in (1, 2, 4):
            run = run + jnp.where(sub >= by, power * pltpu.roll(run, by, 0), 0.0)
            power = power * power
        total_ref[m : m + 1, :] = run[SEGS - 1 : SEGS, :]
        carry_ref[m] = jnp.where(sub >= 1, pltpu.roll(run, 1, 0), 0.0)


def finish_kernel(seg_len, modes, y_ref, qf_ref, carry_ref, entering_ref, rates_ref, res_ref, hidden_ref, rows_ref):
    wide = (SEGS, LANES)
    sub = lax.broadcasted_iota(jnp.int32, wide, 0).astype(jnp.float32)
    rates = rates_ref[...]
    pole = jnp.exp(-rates)
    poles, starts = [], []
    for m in range(modes):
        rate = jnp.broadcast_to(rates[m : m + 1, :], wide)
        come = jnp.exp(-float(seg_len) * sub * rate) * jnp.broadcast_to(entering_ref[m : m + 1, :], wide)
        poles.append(jnp.broadcast_to(pole[m : m + 1, :], wide))
        starts.append(jnp.broadcast_to(res_ref[m : m + 1, :], wide) * (carry_ref[m] + come))

    def step(j, states):
        parts = [y_ref[j], None, None, None]
        new_states = []
        for m in range(modes):
            state = poles[m] * states[m]
            new_states.append(state)
            parts[m % 4] = state if parts[m % 4] is None else parts[m % 4] + state
        rows_ref[pl.ds(j, SEGS, stride=seg_len), :] = qf_ref[j] * ((parts[0] + parts[1]) + (parts[2] + parts[3]))
        return tuple(new_states)

    lax.fori_loop(0, seg_len, step, tuple(starts), unroll=4)
    hidden_ref[...] = rows_ref[...].astype(jnp.bfloat16)


def tail_kernel(q_ref, k_ref, v_ref, out_ref):
    out_ref[0:8, :] = q_ref[...]
    out_ref[8:16, :] = k_ref[...]
    out_ref[16:24, :] = v_ref[...]


def last_tokens(q, k, v):
    rows, channels = q.shape
    last = pl.BlockSpec((8, channels), lambda i: (rows // 8 - 1, 0))
    return pl.pallas_call(
        tail_kernel,
        grid=(1,),
        in_specs=[last] * 3,
        out_specs=pl.BlockSpec((24, channels), lambda i: (0, 0)),
        out_shape=jax.ShapeDtypeStruct((24, channels), jnp.float32),
        compiler_params=pltpu.CompilerParams(vmem_limit_bytes=56 * 2**20),
        cost_estimate=pl.CostEstimate(flops=0, bytes_accessed=0, transcendentals=0),
        name="last_tokens",
    )(q, k, v)


def local_part(q, k, v, halo, taps, rates, res, skip):
    rows, channels = q.shape
    modes = rates.shape[0]
    seg_len = rows // SEGS
    tall = pl.BlockSpec((rows, LANES), lambda c: (0, c))

    def short(n):
        return pl.BlockSpec((n, LANES), lambda c: (0, c))

    cube = pl.BlockSpec((seg_len, SEGS, LANES), lambda c: (0, 0, c))
    mode_cube = pl.BlockSpec((modes, SEGS, LANES), lambda c: (0, 0, c))
    f32 = jnp.float32
    return pl.pallas_call(
        functools.partial(local_kernel, seg_len, modes),
        grid=(channels // LANES,),
        in_specs=[tall, tall, tall, short(24), pl.BlockSpec((3, 3, LANES), lambda c: (0, 0, c)), short(modes), short(modes), short(1)],
        out_specs=[cube, cube, short(modes), mode_cube],
        out_shape=[
            jax.ShapeDtypeStruct((seg_len, SEGS, channels), f32),
            jax.ShapeDtypeStruct((seg_len, SEGS, channels), f32),
            jax.ShapeDtypeStruct((modes, channels), f32),
            jax.ShapeDtypeStruct((modes, SEGS, channels), f32),
        ],
        compiler_params=pltpu.CompilerParams(vmem_limit_bytes=56 * 2**20),
        cost_estimate=pl.CostEstimate(flops=0, bytes_accessed=0, transcendentals=0),
        name="local_part",
    )(q, k, v, halo, taps, rates, res, skip)


def finish_part(y, qf, carry, entering, rates, res):
    seg_len, _, channels = y.shape
    modes = rates.shape[0]
    rows = seg_len * SEGS

    def short(n):
        return pl.BlockSpec((n, LANES), lambda c: (0, c))

    cube = pl.BlockSpec((seg_len, SEGS, LANES), lambda c: (0, 0, c))
    mode_cube = pl.BlockSpec((modes, SEGS, LANES), lambda c: (0, 0, c))
    return pl.pallas_call(
        functools.partial(finish_kernel, seg_len, modes),
        grid=(channels // LANES,),
        in_specs=[cube, cube, mode_cube, short(modes), short(modes), short(modes)],
        out_specs=pl.BlockSpec((rows, LANES), lambda c: (0, c)),
        out_shape=jax.ShapeDtypeStruct((rows, channels), jnp.bfloat16),
        scratch_shapes=[pltpu.VMEM((rows, LANES), jnp.float32)],
        compiler_params=pltpu.CompilerParams(vmem_limit_bytes=56 * 2**20),
        cost_estimate=pl.CostEstimate(flops=0, bytes_accessed=0, transcendentals=0),
        name="finish_part",
    )(y, qf, carry, entering, rates, res)


def pick(first, second):
    return jnp.where(lax.axis_index("core") == 0, first, second)


def entering_state(total, decay, also):
    core, x, zl = lax.axis_index("core"), lax.axis_index("x"), lax.axis_index("zl")
    beside = moved(total, "core", 1)
    chip = jnp.where(core == 0, decay(1) * total + beside, decay(1) * beside + total)
    near = jnp.zeros_like(total)
    plane = decay(2 * (3 - x)) * chip
    for back in (1, 2, 3):
        came = moved(chip, "x", back)
        near = near + jnp.where(x >= back, decay(2 * back - 2) * came, 0.0)
        plane = plane + decay(2 * (3 - (x - back) % 4)) * came
    plane, also = tie(plane, also)
    before = moved(plane, "zl", 1)
    at_chip = near + jnp.where(zl == 1, decay(2 * x) * before, 0.0)
    return jnp.where(core == 0, at_chip, decay(1) * at_chip + beside), also


def on_device(q, k, v, short_taps, rates, res, skip, weight):
    channels = rates.shape[1]
    rows = q.shape[0]
    tails = last_tokens(q, k, v)
    ctx_at = lax.axis_index(CTX)

    def onto_next(at):
        index = (place(CTX, at) + 1) % 16
        return {"zl": index // 8, "x": index // 2 % 4, "core": index % 2}

    halo, weight = tie(permute(tails, CTX, onto_next), weight)
    halo = jnp.where(ctx_at == 0, 0.0, halo)
    block = turned(weight)
    y, qf, total, carry = local_part(
        q, k, v, halo, short_taps, rates, res, skip.reshape(1, channels)
    )

    def decay(times):
        return jnp.exp(-rates * jnp.asarray(rows * times, jnp.float32))

    def turn_x(block):
        return onward(block, "x")

    def turn_y(block):
        return onward(block, "y")

    def across(block):
        return moved(block, "zl", 1)

    def swap(block):
        return moved(block, "core", 1)

    entering, block = entering_state(total, decay, block)
    w, s, h = {(0, 0): block}, {}, {}
    w[0, 1] = turn_x(block)
    hidden = finish_part(y, qf, carry, entering, rates, res)

    hidden, w[0, 1] = tie(hidden, w[0, 1])
    h[0, 0] = hidden
    plus, minus = moved(hidden, "y", 1), moved(hidden, "y", -1)
    h[1, 0] = moved(hidden, "zh", 1)
    w[1, 0] = across(block)
    w[0, 2] = turn_x(w[0, 1])

    plus, minus, h[1, 0], w[1, 0], w[0, 2] = tie(plus, minus, h[1, 0], w[1, 0], w[0, 2])
    h[0, 1], h[0, 3] = plus, minus
    h[0, 2] = onward(pick(plus, minus), "y")
    plus, minus = moved(h[1, 0], "y", 1), moved(h[1, 0], "y", -1)
    w[0, 3] = turn_x(w[0, 2])
    w[1, 1] = turn_x(w[1, 0])

    plus, minus, h[0, 2], w[0, 1], w[0, 2], w[0, 3], w[1, 0], w[1, 1] = tie(
        plus, minus, h[0, 2], w[0, 1], w[0, 2], w[0, 3], w[1, 0], w[1, 1]
    )
    w[1, 3] = across(w[0, 3])
    w[1, 2] = turn_x(w[1, 1])
    for at in ((0, 0), (0, 1), (0, 2), (0, 3), (1, 0), (1, 1)):
        s[at] = swap(w[at])
    h[1, 1], h[1, 3] = plus, minus
    h[1, 2] = onward(pick(plus, minus), "y")
    for at in ((1, 2), (1, 3)):
        s[at] = swap(w[at])

    slots = [(a, b) for a in (0, 1) for b in range(4)]
    late = h[1, 2]
    held = jnp.stack([jnp.zeros_like(late) if at == (1, 2) else h[at] for at in slots])
    flip = (lax.axis_index("zh") + lax.axis_index("zl")) % 2
    apart = lax.axis_index("y") - lax.axis_index("x")
    sign = jnp.where(lax.axis_index("core") == 0, 1, -1)
    own = jnp.zeros((rows, weight.shape[1]), jnp.float32)
    other = jnp.zeros((rows, weight.shape[1]), jnp.float32)

    def dot(a, b):
        return jnp.dot(a, b, preferred_element_type=jnp.float32)

    def term(a, b):
        slot = ((a + flip) % 2) * 4 + (-apart - b) % 4
        return lax.dynamic_index_in_dim(held, slot, 0, keepdims=False)

    for a, b in slots:
        own = own + dot(term(a, sign * b), w[a, b])
        other = other + dot(term(a, -sign * b), s[a, b])

    def add_late(at_own, at_other):
        def add(own, other, late):
            return own + dot(late, w[at_own]), other + dot(late, s[at_other])

        return add

    plane = (1 + flip) % 2
    ring = (-apart - 2) % 4
    branches = [add_late((a, b), (a, (-b) % 4)) for a in (0, 1) for b in range(4)]
    own, other = lax.switch(plane * 4 + (sign * ring) % 4, branches, own, other, late)
    first = lax.axis_index("core") == 0
    return jnp.concatenate([jnp.where(first, own, other), jnp.where(first, other, own)], axis=1)


def solution(mesh):
    fine = Mesh(mesh.devices.reshape(tuple(SIZES[a] for a in AXES)), AXES)
    in_specs = (
        P(CTX, TP),
        P(CTX, TP),
        P(CTX, TP),
        P(None, None, TP),
        P(None, TP),
        P(None, TP),
        P(TP),
        P(TP, CTX),
    )
    return jax.shard_map(on_device, mesh=fine, in_specs=in_specs, out_specs=P(CTX, TP), check_vma=False)
```

```python
import functools
import itertools

import jax
import jax.numpy as jnp
from jax import lax
from jax.experimental import pallas as pl
from jax.experimental.pallas import tpu as pltpu
from jax.sharding import Mesh, PartitionSpec as P

AXES = ("zl", "x", "core", "zh", "y")
SIZES = {"zl": 2, "x": 4, "core": 2, "zh": 2, "y": 4}
CTX = ("zl", "x", "core")
TP = ("zh", "y")
SEGS = 8
LANES = 128
LOCAL_BYTES = 0


def coords(axes):
    for values in itertools.product(*[range(SIZES[a]) for a in axes]):
        yield dict(zip(axes, values))


def place(axes, at):
    index = 0
    for a in axes:
        index = index * SIZES[a] + at[a]
    return index


def permute(value, axes, move):
    pairs = [(place(axes, at), place(axes, move(at))) for at in coords(axes)]
    return lax.ppermute(value, axes, pairs)


def moved(value, axis, by):
    return permute(value, (axis,), lambda at: {axis: (at[axis] + by) % SIZES[axis]})


def onward(value, axis):
    axes = tuple(a for a in AXES if a in (axis, "core"))

    def move(at):
        step = 1 if at["core"] == 0 else -1
        return {**at, axis: (at[axis] + step) % SIZES[axis]}

    return permute(value, axes, move)


def turned(value):
    def move(at):
        return {
            "zl": at["zh"],
            "x": (2 * at["x"] - at["y"]) % 4,
            "core": at["core"],
            "zh": at["zl"],
            "y": at["x"],
        }

    return permute(value, AXES, move)


def tie(*values):
    return lax.optimization_barrier(values)


def local_kernel(seg_len, modes, tiles, q_hbm, k_hbm, v_hbm, halo_ref, taps_ref, rates_ref, res_ref, skip_ref, y_ref, qf_ref, total_ref, carry_ref, buffer, arrived):
    wide = (SEGS, LANES)
    sub = lax.broadcasted_iota(jnp.int32, wide, 0)
    sources = (q_hbm, k_hbm, v_hbm)

    def copy_in(a, c):
        lanes = pl.ds(c * LANES, LANES)
        return pltpu.make_async_copy(sources[a].at[:, lanes], buffer.at[a, c], arrived.at[a, c])

    for c in range(tiles):
        for a in range(3):
            copy_in(a, c).start()

    def spread(row):
        return jnp.broadcast_to(row, wide)

    def tile(c, nothing):
        for a in range(3):
            copy_in(a, c).wait()
        lanes = pl.ds(pl.multiple_of(c * LANES, LANES), LANES)
        rates = rates_ref[:, lanes]
        pole = jnp.exp(-rates)
        gain = res_ref[:, lanes]
        taps = [[spread(taps_ref[a, b : b + 1, lanes]) for b in range(3)] for a in range(3)]
        skip = spread(skip_ref[:, lanes])
        poles = [spread(pole[m : m + 1, :]) for m in range(modes)]
        gains = [spread(gain[m : m + 1, :]) for m in range(modes)]

        def rows_at(a, j):
            return buffer[a, c, pl.ds(j, SEGS, stride=seg_len), :]

        def before(a, back):
            row = 8 * a + 8 - back
            rolled = pltpu.roll(rows_at(a, seg_len - back), 1, 0)
            return jnp.where(sub == 0, spread(halo_ref[row : row + 1, lanes]), rolled)

        def step(j, carried):
            past, states = carried
            feats, new_past = [], []
            for a in range(3):
                now = rows_at(a, j)
                one, two = past[a]
                feats.append(taps[a][0] * now + taps[a][1] * one + taps[a][2] * two)
                new_past.append((now, one))
            gated = feats[1] * feats[2]
            parts = [skip * gated, None, None, None]
            new_states = []
            for m in range(modes):
                state = poles[m] * states[m] + gated
                new_states.append(state)
                term = gains[m] * state
                parts[m % 4] = term if parts[m % 4] is None else parts[m % 4] + term
            y_ref[j, :, lanes] = (parts[0] + parts[1]) + (parts[2] + parts[3])
            qf_ref[j, :, lanes] = feats[0]
            return tuple(new_past), tuple(new_states)

        past = tuple((before(a, 1), before(a, 2)) for a in range(3))
        zeros = tuple(jnp.zeros(wide, jnp.float32) for _ in range(modes))
        _, ends = lax.fori_loop(0, seg_len, step, (past, zeros), unroll=4)

        seg = jnp.exp(-float(seg_len) * rates)
        for m in range(modes):
            power = spread(seg[m : m + 1, :])
            run = ends[m]
            for by in (1, 2, 4):
                run = run + jnp.where(sub >= by, power * pltpu.roll(run, by, 0), 0.0)
                power = power * power
            total_ref[m : m + 1, lanes] = run[SEGS - 1 : SEGS, :]
            carry_ref[m, :, lanes] = jnp.where(sub >= 1, pltpu.roll(run, 1, 0), 0.0)
        return nothing

    lax.fori_loop(0, tiles, tile, 0)


def finish_kernel(seg_len, modes, y_ref, qf_ref, carry_ref, entering_ref, rates_ref, res_ref, hidden_ref, rows_ref):
    wide = (SEGS, LANES)
    sub = lax.broadcasted_iota(jnp.int32, wide, 0).astype(jnp.float32)
    rates = rates_ref[...]
    pole = jnp.exp(-rates)
    poles, starts = [], []
    for m in range(modes):
        rate = jnp.broadcast_to(rates[m : m + 1, :], wide)
        come = jnp.exp(-float(seg_len) * sub * rate) * jnp.broadcast_to(entering_ref[m : m + 1, :], wide)
        poles.append(jnp.broadcast_to(pole[m : m + 1, :], wide))
        starts.append(jnp.broadcast_to(res_ref[m : m + 1, :], wide) * (carry_ref[m] + come))

    def step(j, states):
        parts = [y_ref[j], None, None, None]
        new_states = []
        for m in range(modes):
            state = poles[m] * states[m]
            new_states.append(state)
            parts[m % 4] = state if parts[m % 4] is None else parts[m % 4] + state
        rows_ref[pl.ds(j, SEGS, stride=seg_len), :] = qf_ref[j] * ((parts[0] + parts[1]) + (parts[2] + parts[3]))
        return tuple(new_states)

    lax.fori_loop(0, seg_len, step, tuple(starts), unroll=4)
    hidden_ref[...] = rows_ref[...].astype(jnp.bfloat16)


def tail_kernel(q_ref, k_ref, v_ref, out_ref):
    out_ref[0:8, :] = q_ref[...]
    out_ref[8:16, :] = k_ref[...]
    out_ref[16:24, :] = v_ref[...]


def last_tokens(q, k, v):
    rows, channels = q.shape
    last = pl.BlockSpec((8, channels), lambda i: (rows // 8 - 1, 0))
    return pl.pallas_call(
        tail_kernel,
        grid=(1,),
        in_specs=[last] * 3,
        out_specs=pl.BlockSpec((24, channels), lambda i: (0, 0)),
        out_shape=jax.ShapeDtypeStruct((24, channels), jnp.float32),
        compiler_params=pltpu.CompilerParams(vmem_limit_bytes=56 * 2**20),
        cost_estimate=pl.CostEstimate(flops=0, bytes_accessed=0, transcendentals=0),
        name="last_tokens",
    )(q, k, v)


def local_part(q, k, v, halo, taps, rates, res, skip):
    rows, channels = q.shape
    modes = rates.shape[0]
    seg_len = rows // SEGS
    tiles = channels // LANES
    f32 = jnp.float32
    outside = pl.BlockSpec(memory_space=pltpu.HBM)
    inside = pl.BlockSpec(memory_space=pltpu.VMEM)
    return pl.pallas_call(
        functools.partial(local_kernel, seg_len, modes, tiles),
        in_specs=[outside] * 3 + [inside] * 5,
        out_specs=[inside] * 4,
        out_shape=[
            jax.ShapeDtypeStruct((seg_len, SEGS, channels), f32),
            jax.ShapeDtypeStruct((seg_len, SEGS, channels), f32),
            jax.ShapeDtypeStruct((modes, channels), f32),
            jax.ShapeDtypeStruct((modes, SEGS, channels), f32),
        ],
        scratch_shapes=[pltpu.VMEM((3, tiles, rows, LANES), f32), pltpu.SemaphoreType.DMA((3, tiles))],
        compiler_params=pltpu.CompilerParams(vmem_limit_bytes=20 * 2**20),
        cost_estimate=pl.CostEstimate(flops=0, bytes_accessed=LOCAL_BYTES, transcendentals=0),
        name="local_part",
    )(q, k, v, halo, taps, rates, res, skip)


def finish_part(y, qf, carry, entering, rates, res):
    seg_len, _, channels = y.shape
    modes = rates.shape[0]
    rows = seg_len * SEGS

    def short(n):
        return pl.BlockSpec((n, LANES), lambda c: (0, c))

    cube = pl.BlockSpec((seg_len, SEGS, LANES), lambda c: (0, 0, c))
    mode_cube = pl.BlockSpec((modes, SEGS, LANES), lambda c: (0, 0, c))
    return pl.pallas_call(
        functools.partial(finish_kernel, seg_len, modes),
        grid=(channels // LANES,),
        in_specs=[cube, cube, mode_cube, short(modes), short(modes), short(modes)],
        out_specs=pl.BlockSpec((rows, LANES), lambda c: (0, c)),
        out_shape=jax.ShapeDtypeStruct((rows, channels), jnp.bfloat16),
        scratch_shapes=[pltpu.VMEM((rows, LANES), jnp.float32)],
        compiler_params=pltpu.CompilerParams(vmem_limit_bytes=20 * 2**20),
        cost_estimate=pl.CostEstimate(flops=0, bytes_accessed=0, transcendentals=0),
        name="finish_part",
    )(y, qf, carry, entering, rates, res)


def pick(first, second):
    return jnp.where(lax.axis_index("core") == 0, first, second)


def entering_state(total, decay, also):
    core, x, zl = lax.axis_index("core"), lax.axis_index("x"), lax.axis_index("zl")
    beside = moved(total, "core", 1)
    chip = jnp.where(core == 0, decay(1) * total + beside, decay(1) * beside + total)
    near = jnp.zeros_like(total)
    plane = decay(2 * (3 - x)) * chip
    for back in (1, 2, 3):
        came = moved(chip, "x", back)
        near = near + jnp.where(x >= back, decay(2 * back - 2) * came, 0.0)
        plane = plane + decay(2 * (3 - (x - back) % 4)) * came
    plane, also = tie(plane, also)
    before, later = tie(moved(plane, "zl", 1), also)
    at_chip = near + jnp.where(zl == 1, decay(2 * x) * before, 0.0)
    return jnp.where(core == 0, at_chip, decay(1) * at_chip + beside), also, later


def on_device(q, k, v, short_taps, rates, res, skip, weight):
    channels = rates.shape[1]
    rows = q.shape[0]
    tails = last_tokens(q, k, v)
    ctx_at = lax.axis_index(CTX)

    def onto_next(at):
        index = (place(CTX, at) + 1) % 16
        return {"zl": index // 8, "x": index // 2 % 4, "core": index % 2}

    halo, weight = tie(permute(tails, CTX, onto_next), weight)
    halo = jnp.where(ctx_at == 0, 0.0, halo)
    block = turned(weight)
    y, qf, total, carry = local_part(
        q, k, v, halo, short_taps, rates, res, skip.reshape(1, channels)
    )

    def decay(times):
        return jnp.exp(-rates * jnp.asarray(rows * times, jnp.float32))

    def turn_x(block):
        return onward(block, "x")

    def turn_y(block):
        return onward(block, "y")

    def across(block):
        return moved(block, "zl", 1)

    def swap(block):
        return moved(block, "core", 1)

    entering, block, block_later = entering_state(total, decay, block)
    w, s, h = {(0, 0): block}, {}, {}
    w[0, 1] = turn_x(block)
    hidden = finish_part(y, qf, carry, entering, rates, res)

    s[0, 0] = swap(block_later)
    hidden, w[0, 1], s[0, 0] = tie(hidden, w[0, 1], s[0, 0])
    h[0, 0] = hidden
    plus, minus = moved(hidden, "y", 1), moved(hidden, "y", -1)
    h[1, 0] = moved(hidden, "zh", 1)
    w[1, 0] = across(block_later)
    w[0, 2] = turn_x(w[0, 1])

    w[1, 1] = turn_x(w[1, 0])

    plus, minus, h[1, 0], w[1, 0], w[0, 2], w[1, 1] = tie(plus, minus, h[1, 0], w[1, 0], w[0, 2], w[1, 1])
    h[0, 1], h[0, 3] = plus, minus
    held = jnp.zeros((8, *hidden.shape), hidden.dtype)
    for at in ((0, 0), (0, 1), (0, 3), (1, 0)):
        held = held.at[at[0] * 4 + at[1]].set(h[at])
    h[0, 2] = onward(pick(plus, minus), "y")
    plus, minus = moved(h[1, 0], "y", 1), moved(h[1, 0], "y", -1)
    w[0, 3] = turn_x(w[0, 2])
    w[1, 2] = turn_x(w[1, 1])

    plus, minus, h[0, 2], w[0, 3], w[1, 2], w[0, 1], w[0, 2], w[1, 0], w[1, 1] = tie(
        plus, minus, h[0, 2], w[0, 3], w[1, 2], w[0, 1], w[0, 2], w[1, 0], w[1, 1]
    )
    next_on = pick(plus, minus)
    next_on, plus, minus, h[0, 2], held = tie(next_on, plus, minus, h[0, 2], held)
    h[1, 1], h[1, 3] = plus, minus
    h[1, 2] = onward(next_on, "y")
    w[1, 3] = turn_x(w[1, 2])
    for at in ((0, 1), (0, 2), (1, 0)):
        s[at] = swap(w[at])
    h[1, 2], w[0, 3], w[1, 1], w[1, 2] = tie(h[1, 2], w[0, 3], w[1, 1], w[1, 2])
    for at in ((0, 3), (1, 1), (1, 2), (1, 3)):
        s[at] = swap(w[at])

    slots = [(a, b) for a in (0, 1) for b in range(4)]
    late = h[1, 2]
    for at in ((0, 2), (1, 1), (1, 3)):
        held = held.at[at[0] * 4 + at[1]].set(h[at])
    flip = (lax.axis_index("zh") + lax.axis_index("zl")) % 2
    apart = lax.axis_index("y") - lax.axis_index("x")
    sign = jnp.where(lax.axis_index("core") == 0, 1, -1)
    own = jnp.zeros((rows, weight.shape[1]), jnp.float32)
    other = jnp.zeros((rows, weight.shape[1]), jnp.float32)

    def dot(a, b):
        return jnp.dot(a, b, preferred_element_type=jnp.float32)

    def term(a, b):
        slot = ((a + flip) % 2) * 4 + (-apart - b) % 4
        return lax.dynamic_index_in_dim(held, slot, 0, keepdims=False)

    for a, b in slots:
        own = own + dot(term(a, sign * b), w[a, b])
        other = other + dot(term(a, -sign * b), s[a, b])

    def add_late(at_own, at_other):
        def add(own, other, late):
            return own + dot(late, w[at_own]), other + dot(late, s[at_other])

        return add

    plane = (1 + flip) % 2
    ring = (-apart - 2) % 4
    branches = [add_late((a, b), (a, (-b) % 4)) for a in (0, 1) for b in range(4)]
    own, other = lax.switch(plane * 4 + (sign * ring) % 4, branches, own, other, late)
    first = lax.axis_index("core") == 0
    return jnp.concatenate([jnp.where(first, own, other), jnp.where(first, other, own)], axis=1)


def solution(mesh):
    fine = Mesh(mesh.devices.reshape(tuple(SIZES[a] for a in AXES)), AXES)
    in_specs = (
        P(CTX, TP),
        P(CTX, TP),
        P(CTX, TP),
        P(None, None, TP),
        P(None, TP),
        P(None, TP),
        P(TP),
        P(TP, CTX),
    )
    return jax.shard_map(on_device, mesh=fine, in_specs=in_specs, out_specs=P(CTX, TP), check_vma=False)
```

```python
import functools
import itertools

import jax
import jax.numpy as jnp
from jax import lax
from jax.experimental import pallas as pl
from jax.experimental.pallas import tpu as pltpu
from jax.sharding import Mesh, PartitionSpec as P

AXES = ("zl", "x", "core", "zh", "y")
SIZES = {"zl": 2, "x": 4, "core": 2, "zh": 2, "y": 4}
CTX = ("zl", "x", "core")
TP = ("zh", "y")
SEGS = 8
LANES = 128
LOCAL_BYTES = 0


def coords(axes):
    for values in itertools.product(*[range(SIZES[a]) for a in axes]):
        yield dict(zip(axes, values))


def place(axes, at):
    index = 0
    for a in axes:
        index = index * SIZES[a] + at[a]
    return index


def permute(value, axes, move):
    pairs = [(place(axes, at), place(axes, move(at))) for at in coords(axes)]
    return lax.ppermute(value, axes, pairs)


def moved(value, axis, by):
    return permute(value, (axis,), lambda at: {axis: (at[axis] + by) % SIZES[axis]})


def onward(value, axis):
    axes = tuple(a for a in AXES if a in (axis, "core"))

    def move(at):
        step = 1 if at["core"] == 0 else -1
        return {**at, axis: (at[axis] + step) % SIZES[axis]}

    return permute(value, axes, move)


def turned(value):
    def move(at):
        return {
            "zl": at["zh"],
            "x": (2 * at["x"] - at["y"]) % 4,
            "core": at["core"],
            "zh": at["zl"],
            "y": at["x"],
        }

    return permute(value, AXES, move)


def tie(*values):
    return lax.optimization_barrier(values)


def local_kernel(seg_len, modes, tiles, q_hbm, k_hbm, v_hbm, halo_ref, taps_ref, rates_ref, res_ref, skip_ref, y_ref, qf_ref, total_ref, carry_ref, buffer, arrived):
    wide = (SEGS, LANES)
    sub = lax.broadcasted_iota(jnp.int32, wide, 0)
    sources = (q_hbm, k_hbm, v_hbm)

    def copy_in(a, c):
        lanes = pl.ds(c * LANES, LANES)
        return pltpu.make_async_copy(sources[a].at[:, lanes], buffer.at[a, c], arrived.at[a, c])

    for c in range(tiles):
        for a in range(3):
            copy_in(a, c).start()

    def spread(row):
        return jnp.broadcast_to(row, wide)

    def tile(c, nothing):
        for a in range(3):
            copy_in(a, c).wait()
        lanes = pl.ds(pl.multiple_of(c * LANES, LANES), LANES)
        rates = rates_ref[:, lanes]
        pole = jnp.exp(-rates)
        gain = res_ref[:, lanes]
        taps = [[spread(taps_ref[a, b : b + 1, lanes]) for b in range(3)] for a in range(3)]
        skip = spread(skip_ref[:, lanes])
        poles = [spread(pole[m : m + 1, :]) for m in range(modes)]
        gains = [spread(gain[m : m + 1, :]) for m in range(modes)]

        def rows_at(a, j):
            return buffer[a, c, pl.ds(j, SEGS, stride=seg_len), :]

        def before(a, back):
            row = 8 * a + 8 - back
            rolled = pltpu.roll(rows_at(a, seg_len - back), 1, 0)
            return jnp.where(sub == 0, spread(halo_ref[row : row + 1, lanes]), rolled)

        def step(j, carried):
            past, states = carried
            feats, new_past = [], []
            for a in range(3):
                now = rows_at(a, j)
                one, two = past[a]
                feats.append(taps[a][0] * now + taps[a][1] * one + taps[a][2] * two)
                new_past.append((now, one))
            gated = feats[1] * feats[2]
            parts = [skip * gated, None, None, None]
            new_states = []
            for m in range(modes):
                state = poles[m] * states[m] + gated
                new_states.append(state)
                term = gains[m] * state
                parts[m % 4] = term if parts[m % 4] is None else parts[m % 4] + term
            y_ref[j, :, lanes] = (parts[0] + parts[1]) + (parts[2] + parts[3])
            qf_ref[j, :, lanes] = feats[0]
            return tuple(new_past), tuple(new_states)

        past = tuple((before(a, 1), before(a, 2)) for a in range(3))
        zeros = tuple(jnp.zeros(wide, jnp.float32) for _ in range(modes))
        _, ends = lax.fori_loop(0, seg_len, step, (past, zeros), unroll=4)

        seg = jnp.exp(-float(seg_len) * rates)
        for m in range(modes):
            power = spread(seg[m : m + 1, :])
            run = ends[m]
            for by in (1, 2, 4):
                run = run + jnp.where(sub >= by, power * pltpu.roll(run, by, 0), 0.0)
                power = power * power
            total_ref[m : m + 1, lanes] = run[SEGS - 1 : SEGS, :]
            carry_ref[m, :, lanes] = jnp.where(sub >= 1, pltpu.roll(run, 1, 0), 0.0)
        return nothing

    lax.fori_loop(0, tiles, tile, 0)


def finish_kernel(seg_len, modes, y_ref, qf_ref, carry_ref, entering_ref, rates_ref, res_ref, hidden_ref, rows_ref):
    wide = (SEGS, LANES)
    sub = lax.broadcasted_iota(jnp.int32, wide, 0).astype(jnp.float32)
    rates = rates_ref[...]
    pole = jnp.exp(-rates)
    poles, starts = [], []
    for m in range(modes):
        rate = jnp.broadcast_to(rates[m : m + 1, :], wide)
        come = jnp.exp(-float(seg_len) * sub * rate) * jnp.broadcast_to(entering_ref[m : m + 1, :], wide)
        poles.append(jnp.broadcast_to(pole[m : m + 1, :], wide))
        starts.append(jnp.broadcast_to(res_ref[m : m + 1, :], wide) * (carry_ref[m] + come))

    def step(j, states):
        parts = [y_ref[j], None, None, None]
        new_states = []
        for m in range(modes):
            state = poles[m] * states[m]
            new_states.append(state)
            parts[m % 4] = state if parts[m % 4] is None else parts[m % 4] + state
        rows_ref[pl.ds(j, SEGS, stride=seg_len), :] = qf_ref[j] * ((parts[0] + parts[1]) + (parts[2] + parts[3]))
        return tuple(new_states)

    lax.fori_loop(0, seg_len, step, tuple(starts), unroll=4)
    hidden_ref[...] = rows_ref[...].astype(jnp.bfloat16)


def tail_kernel(q_ref, k_ref, v_ref, out_ref):
    out_ref[0:8, :] = q_ref[...]
    out_ref[8:16, :] = k_ref[...]
    out_ref[16:24, :] = v_ref[...]


def last_tokens(q, k, v):
    rows, channels = q.shape
    last = pl.BlockSpec((8, channels), lambda i: (rows // 8 - 1, 0))
    return pl.pallas_call(
        tail_kernel,
        grid=(1,),
        in_specs=[last] * 3,
        out_specs=pl.BlockSpec((24, channels), lambda i: (0, 0)),
        out_shape=jax.ShapeDtypeStruct((24, channels), jnp.float32),
        compiler_params=pltpu.CompilerParams(vmem_limit_bytes=56 * 2**20),
        cost_estimate=pl.CostEstimate(flops=0, bytes_accessed=0, transcendentals=0),
        name="last_tokens",
    )(q, k, v)


def local_part(q, k, v, halo, taps, rates, res, skip):
    rows, channels = q.shape
    modes = rates.shape[0]
    seg_len = rows // SEGS
    tiles = channels // LANES
    f32 = jnp.float32
    outside = pl.BlockSpec(memory_space=pltpu.HBM)
    inside = pl.BlockSpec(memory_space=pltpu.VMEM)
    return pl.pallas_call(
        functools.partial(local_kernel, seg_len, modes, tiles),
        in_specs=[outside] * 3 + [inside] * 5,
        out_specs=[inside] * 4,
        out_shape=[
            jax.ShapeDtypeStruct((seg_len, SEGS, channels), f32),
            jax.ShapeDtypeStruct((seg_len, SEGS, channels), f32),
            jax.ShapeDtypeStruct((modes, channels), f32),
            jax.ShapeDtypeStruct((modes, SEGS, channels), f32),
        ],
        scratch_shapes=[pltpu.VMEM((3, tiles, rows, LANES), f32), pltpu.SemaphoreType.DMA((3, tiles))],
        compiler_params=pltpu.CompilerParams(vmem_limit_bytes=20 * 2**20),
        cost_estimate=pl.CostEstimate(flops=0, bytes_accessed=LOCAL_BYTES, transcendentals=0),
        name="local_part",
    )(q, k, v, halo, taps, rates, res, skip)


def finish_part(y, qf, carry, entering, rates, res):
    seg_len, _, channels = y.shape
    modes = rates.shape[0]
    rows = seg_len * SEGS

    def short(n):
        return pl.BlockSpec((n, LANES), lambda c: (0, c))

    cube = pl.BlockSpec((seg_len, SEGS, LANES), lambda c: (0, 0, c))
    mode_cube = pl.BlockSpec((modes, SEGS, LANES), lambda c: (0, 0, c))
    return pl.pallas_call(
        functools.partial(finish_kernel, seg_len, modes),
        grid=(channels // LANES,),
        in_specs=[cube, cube, mode_cube, short(modes), short(modes), short(modes)],
        out_specs=pl.BlockSpec((rows, LANES), lambda c: (0, c)),
        out_shape=jax.ShapeDtypeStruct((rows, channels), jnp.bfloat16),
        scratch_shapes=[pltpu.VMEM((rows, LANES), jnp.float32)],
        compiler_params=pltpu.CompilerParams(vmem_limit_bytes=20 * 2**20),
        cost_estimate=pl.CostEstimate(flops=0, bytes_accessed=0, transcendentals=0),
        name="finish_part",
    )(y, qf, carry, entering, rates, res)


def pick(first, second):
    return jnp.where(lax.axis_index("core") == 0, first, second)


def entering_state(total, decay, also):
    core, x, zl = lax.axis_index("core"), lax.axis_index("x"), lax.axis_index("zl")
    beside = moved(total, "core", 1)
    chip = jnp.where(core == 0, decay(1) * total + beside, decay(1) * beside + total)
    near = jnp.zeros_like(total)
    plane = decay(2 * (3 - x)) * chip
    for back in (1, 2, 3):
        came = moved(chip, "x", back)
        near = near + jnp.where(x >= back, decay(2 * back - 2) * came, 0.0)
        plane = plane + decay(2 * (3 - (x - back) % 4)) * came
    plane, also = tie(plane, also)
    before, later = tie(moved(plane, "zl", 1), also)
    at_chip = near + jnp.where(zl == 1, decay(2 * x) * before, 0.0)
    return jnp.where(core == 0, at_chip, decay(1) * at_chip + beside), also, later


def on_device(q, k, v, short_taps, rates, res, skip, weight):
    channels = rates.shape[1]
    rows = q.shape[0]
    tails = last_tokens(q, k, v)
    ctx_at = lax.axis_index(CTX)

    def onto_next(at):
        index = (place(CTX, at) + 1) % 16
        return {"zl": index // 8, "x": index // 2 % 4, "core": index % 2}

    halo, weight = tie(permute(tails, CTX, onto_next), weight)
    halo = jnp.where(ctx_at == 0, 0.0, halo)
    block = turned(weight)
    y, qf, total, carry = local_part(
        q, k, v, halo, short_taps, rates, res, skip.reshape(1, channels)
    )

    def decay(times):
        return jnp.exp(-rates * jnp.asarray(rows * times, jnp.float32))

    def turn_x(block):
        return onward(block, "x")

    def turn_y(block):
        return onward(block, "y")

    def across(block):
        return moved(block, "zl", 1)

    def swap(block):
        return moved(block, "core", 1)

    entering, block, block_later = entering_state(total, decay, block)
    w, s, h = {(0, 0): block}, {}, {}
    w[0, 1] = turn_x(block)
    hidden = finish_part(y, qf, carry, entering, rates, res)

    s[0, 0] = swap(block_later)
    hidden, w[0, 1], s[0, 0] = tie(hidden, w[0, 1], s[0, 0])
    h[0, 0] = hidden
    plus, minus = moved(hidden, "y", 1), moved(hidden, "y", -1)
    h[1, 0] = moved(hidden, "zh", 1)
    w[1, 0] = across(block_later)
    w[0, 2] = turn_x(w[0, 1])

    w[1, 1] = turn_x(w[1, 0])

    plus, minus, h[1, 0], w[1, 0], w[0, 2], w[1, 1] = tie(plus, minus, h[1, 0], w[1, 0], w[0, 2], w[1, 1])
    h[0, 1], h[0, 3] = plus, minus
    held = jnp.zeros((8, *hidden.shape), hidden.dtype)
    for at in ((0, 0), (0, 1), (0, 3), (1, 0)):
        held = held.at[at[0] * 4 + at[1]].set(h[at])
    h[0, 2] = onward(pick(plus, minus), "y")
    plus, minus = moved(h[1, 0], "y", 1), moved(h[1, 0], "y", -1)
    w[0, 3] = turn_x(w[0, 2])
    w[1, 2] = turn_x(w[1, 1])

    plus, minus, h[0, 2], w[0, 3], w[1, 2], w[0, 1], w[0, 2], w[1, 0], w[1, 1] = tie(
        plus, minus, h[0, 2], w[0, 3], w[1, 2], w[0, 1], w[0, 2], w[1, 0], w[1, 1]
    )
    next_on = pick(plus, minus)
    next_on, plus, minus, h[0, 2], held = tie(next_on, plus, minus, h[0, 2], held)
    h[1, 1], h[1, 3] = plus, minus
    h[1, 2] = onward(next_on, "y")
    w[1, 3] = turn_x(w[1, 2])
    for at in ((0, 1), (0, 2), (1, 0)):
        s[at] = swap(w[at])
    s[0, 1], s[0, 2], s[1, 0], w[0, 3], w[1, 1], w[1, 2] = tie(s[0, 1], s[0, 2], s[1, 0], w[0, 3], w[1, 1], w[1, 2])
    for at in ((0, 3), (1, 1), (1, 2), (1, 3)):
        s[at] = swap(w[at])

    slots = [(a, b) for a in (0, 1) for b in range(4)]
    late = h[1, 2]
    for at in ((0, 2), (1, 1), (1, 3)):
        held = held.at[at[0] * 4 + at[1]].set(h[at])
    flip = (lax.axis_index("zh") + lax.axis_index("zl")) % 2
    apart = lax.axis_index("y") - lax.axis_index("x")
    sign = jnp.where(lax.axis_index("core") == 0, 1, -1)
    own = jnp.zeros((rows, weight.shape[1]), jnp.float32)
    other = jnp.zeros((rows, weight.shape[1]), jnp.float32)

    def dot(a, b):
        return jnp.dot(a, b, preferred_element_type=jnp.float32)

    def term(a, b):
        slot = ((a + flip) % 2) * 4 + (-apart - b) % 4
        return lax.dynamic_index_in_dim(held, slot, 0, keepdims=False)

    for a, b in slots:
        own = own + dot(term(a, sign * b), w[a, b])
        other = other + dot(term(a, -sign * b), s[a, b])

    def add_late(at_own, at_other):
        def add(own, other, late):
            return own + dot(late, w[at_own]), other + dot(late, s[at_other])

        return add

    plane = (1 + flip) % 2
    ring = (-apart - 2) % 4
    branches = [add_late((a, b), (a, (-b) % 4)) for a in (0, 1) for b in range(4)]
    own, other = lax.switch(plane * 4 + (sign * ring) % 4, branches, own, other, late)
    first = lax.axis_index("core") == 0
    return jnp.concatenate([jnp.where(first, own, other), jnp.where(first, other, own)], axis=1)


def solution(mesh):
    fine = Mesh(mesh.devices.reshape(tuple(SIZES[a] for a in AXES)), AXES)
    in_specs = (
        P(CTX, TP),
        P(CTX, TP),
        P(CTX, TP),
        P(None, None, TP),
        P(None, TP),
        P(None, TP),
        P(TP),
        P(TP, CTX),
    )
    return jax.shard_map(on_device, mesh=fine, in_specs=in_specs, out_specs=P(CTX, TP), check_vma=False)
```
